32 devices in a mesh: col: 4 (over y, x), blk: 8 (over z, core).
Axes of the slice: x: 2, y: 2, z: 4, core: 2. Of those that a mesh axis runs over, the one named last changes fastest.
Arguments:
- corner_up: bfloat16 [4, 256, 256], P('col'), may hold values from -0.375 to 0.375
- corner_dn: bfloat16 [4, 256, 256], P('col'), may hold values from -0.375 to 0.375
- edge_top: bfloat16 [4, 256, 36, 256], P('col', 'blk'), may hold values from -6 to 6
- edge_bot: bfloat16 [4, 256, 36, 256], P('col', 'blk'), may hold values from -6 to 6
- edge_up: bfloat16 [4, 256, 36, 256], P('col', 'blk'), may hold values from -0.375 to 0.375
- edge_dn: bfloat16 [4, 256, 36, 256], P('col', 'blk'), may hold values from -0.375 to 0.375
- site_up: bfloat16 [4, 36, 36, 36, 36], P('col'), may hold values from -0.15625 to 0.15625
- site_dn: bfloat16 [4, 36, 36, 36, 36], P('col'), may hold values from -0.15625 to 0.15625
- proj_up: bfloat16 [4, 9216, 256], P('col', 'blk'), may hold values from -0.0625 to 0.0625
- proj_dn: bfloat16 [4, 9216, 256], P('col', 'blk'), may hold values from -0.0625 to 0.0625
Outputs:
- half_proj: bfloat16 [4, 9216, 256], P('col', 'blk')
- next_up: bfloat16 [4, 256, 256], P('col', 'blk')
- next_dn: bfloat16 [4, 256, 256], P('col', 'blk')
The draws below stay inside these ranges and needn't reach their ends.
All inputs are finite; a program needn't handle non-finite values.
Results may differ from the reference program's by a relative error of at most 0.018.
Values may be sent and summed in bfloat16 or wider, within the bound.
No kernel may reach another device: no remote copies, remote signals or barrier semaphores. Data moves between devices by JAX's collectives and lax.ppermute only.
A program may use at most 128 MiB of HBM per device.

```python
import jax
import jax.numpy as jnp
from jax import lax

CHI = 256
D2 = 36
COLS = 4


def steps_of(rng, dims, cuts, low, largest):
    level = 1.0
    for position, parts in cuts:
        steps = jax.random.uniform(jax.random.fold_in(jax.random.fold_in(rng, 6), position), (parts,), jnp.float32, low / len(cuts), largest / len(cuts))
        level = level * jnp.repeat(jnp.exp(steps), dims[position] // parts).reshape((-1,) + (1,) * (len(dims) - 1 - position))
    return level


def normal_values(stream_key, extent, deviation, bound, pieces=(), dtype=jnp.bfloat16):
    drawn = deviation * jax.random.normal(stream_key, extent, jnp.float32)
    if pieces:
        drawn = drawn * steps_of(stream_key, extent, pieces, -0.22, 0.18)
    return jnp.clip(drawn, -bound, bound).astype(dtype)


def setup_inputs(seed: int = 0) -> dict:
    key_list = jax.random.split(jax.random.key(seed), 11)
    corner_up = normal_values(key_list[0], (COLS, CHI, CHI), CHI ** -0.5, 0.375, ((0, 4),))
    corner_dn = normal_values(key_list[1], (COLS, CHI, CHI), CHI ** -0.5, 0.375, ((0, 4),))
    edge_top = normal_values(key_list[2], (COLS, CHI, D2, CHI), 1.0, 6.0, ((0, 4), (1, 8)))
    edge_bot = normal_values(key_list[3], (COLS, CHI, D2, CHI), 1.0, 6.0, ((0, 4), (1, 8)))
    edge_up = normal_values(key_list[4], (COLS, CHI, D2, CHI), CHI ** -0.5, 0.375, ((0, 4), (1, 8)))
    edge_dn = normal_values(key_list[5], (COLS, CHI, D2, CHI), CHI ** -0.5, 0.375, ((0, 4), (1, 8)))
    site_up = normal_values(key_list[6], (COLS, D2, D2, D2, D2), (D2 * D2) ** -0.5, 0.15625, ((0, 4),))
    site_dn = normal_values(key_list[7], (COLS, D2, D2, D2, D2), (D2 * D2) ** -0.5, 0.15625, ((0, 4),))
    proj_up = normal_values(key_list[8], (COLS, CHI * D2, CHI), (CHI * D2) ** -0.5, 0.0625, ((0, 4), (1, 8)))
    proj_dn = normal_values(key_list[9], (COLS, CHI * D2, CHI), (CHI * D2) ** -0.5, 0.0625, ((0, 4), (1, 8)))
    return {"corner_up": corner_up, "corner_dn": corner_dn, "edge_top": edge_top, "edge_bot": edge_bot, "edge_up": edge_up, "edge_dn": edge_dn, "site_up": site_up, "site_dn": site_dn, "proj_up": proj_up, "proj_dn": proj_dn}


def enlarge(edge, grown, site):
    rows = edge.shape[0]
    wide = jnp.dot(edge.reshape(rows * D2, CHI), grown, preferred_element_type=jnp.float32).astype(jnp.bfloat16)
    wide = wide.reshape(rows, D2 * D2, CHI)
    table = site.transpose(2, 1, 3, 0).reshape(D2 * D2, D2 * D2)
    block = jnp.einsum("ab,ibj->iaj", table.astype(jnp.float32), wide.astype(jnp.float32)).astype(jnp.bfloat16)
    return block.reshape(rows * D2, D2 * CHI)


def column(items):
    c_up, c_dn, top, bot, e_up, e_dn, s_up, s_dn, p_up, p_dn = items
    grown_up = jnp.dot(c_up, top.reshape(CHI, D2 * CHI), preferred_element_type=jnp.float32).astype(jnp.bfloat16)
    grown_dn = jnp.dot(c_dn, bot.reshape(CHI, D2 * CHI), preferred_element_type=jnp.float32).astype(jnp.bfloat16)
    quad_up = enlarge(e_up, grown_up, s_up)
    quad_dn = enlarge(e_dn, grown_dn, s_dn)
    cut = lax.dot_general(quad_dn, p_dn, (((0,), (0,)), ((), ())), preferred_element_type=jnp.float32).astype(jnp.bfloat16)
    half = jnp.dot(quad_up, cut, preferred_element_type=jnp.float32) * (1.0 / (CHI * D2) ** 0.5)
    fresh_up = lax.dot_general(p_up, grown_up.reshape(CHI * D2, CHI), (((0,), (0,)), ((), ())), preferred_element_type=jnp.float32).astype(jnp.bfloat16)
    fresh_dn = lax.dot_general(p_dn, grown_dn.reshape(CHI * D2, CHI), (((0,), (0,)), ((), ())), preferred_element_type=jnp.float32).astype(jnp.bfloat16)
    return half.astype(jnp.bfloat16), fresh_up, fresh_dn


def reference(corner_up, corner_dn, edge_top, edge_bot, edge_up, edge_dn, site_up, site_dn, proj_up, proj_dn):
    half_proj, fresh_up, fresh_dn = lax.map(column, (corner_up, corner_dn, edge_top, edge_bot, edge_up, edge_dn, site_up, site_dn, proj_up, proj_dn))
    return half_proj, jnp.roll(fresh_up, 1, axis=0), jnp.roll(fresh_dn, 1, axis=0)
```

```python
import functools

import jax
import jax.numpy as jnp
from jax import lax
from jax.experimental import pallas as pl
from jax.experimental.pallas import tpu as pltpu
from jax.sharding import PartitionSpec as P

BF = jnp.bfloat16
F32 = jnp.float32
LANES = 128
VMEM = 56 * 1024 * 1024


def round_up(value, step):
    return (value + step - 1) // step * step


def params():
    return pltpu.CompilerParams(vmem_limit_bytes=VMEM)


def cost(flops, moved):
    return pl.CostEstimate(flops=int(flops), bytes_accessed=int(moved), transcendentals=0)


def table_kernel(width, vp, per, body, site_ref, out_ref):
    part = site_ref.shape[1]
    tail = width - body

    def one_group(g, carry):
        lane = pl.ds(pl.multiple_of(g * LANES, LANES), LANES)
        tails = []
        for t in range(part):
            pieces = []
            for r in range(per):
                pieces.append(site_ref[g * per + r, t].astype(F32))
                gap = vp - width if r < per - 1 else LANES - (per - 1) * vp - width
                pieces.append(jnp.zeros((width, gap), F32))
            full = jnp.concatenate(pieces, axis=1)
            out_ref[0, t * body : (t + 1) * body, lane] = full[:body].astype(BF)
            tails.append(full[body:])
        out_ref[0, part * body :, lane] = jnp.concatenate(tails, axis=0).astype(BF)
        return carry

    lax.fori_loop(0, width // per, one_group, 0)


def make_table(site, vp, per, body):
    width = site.shape[0]
    half = width // 2
    depth = width // per * LANES
    return pl.pallas_call(
        functools.partial(table_kernel, width, vp, per, body),
        grid=(2,),
        in_specs=[pl.BlockSpec((width, half, width, width), lambda h: (0, h, 0, 0))],
        out_specs=pl.BlockSpec((1, half * width, depth), lambda h: (h, 0, 0)),
        out_shape=jax.ShapeDtypeStruct((2, half * width, depth), BF),
        compiler_params=params(),
        cost_estimate=cost(0, 30e6),
        name="table",
    )(site)


def wide_kernel(vp, per, chunk, corner_ref, top_ref, edge_ref, grown_ref, wide_ref):
    legs = top_ref.shape[0]
    weights = []
    for q in range(legs // 2):
        right = jnp.concatenate([top_ref[2 * q], top_ref[2 * q + 1]], axis=1)
        g = jnp.dot(corner_ref[...], right, preferred_element_type=F32).astype(BF)
        grown_ref[q] = g
    pad = jnp.zeros((LANES - per * vp, LANES), F32)
    rows = edge_ref.shape[0] // vp

    def one_chunk(c, carry):
        left = edge_ref[pl.ds(pl.multiple_of(c * chunk * vp, 16), chunk * vp), :]
        res = [
            jnp.dot(left, grown_ref[q], preferred_element_type=F32) for q in range(legs // 2)
        ]
        for k in range(chunk):
            pieces = []
            for u in range(legs):
                lo = (u % 2) * LANES
                pieces.append(res[u // 2][k * vp : (k + 1) * vp, lo : lo + LANES])
                if u % per == per - 1:
                    pieces.append(pad)
            block = jnp.concatenate(pieces, axis=0).astype(BF)
            lo = (k % 2) * LANES
            wide_ref[c * (chunk // 2) + k // 2, :, lo : lo + LANES] = block
        return carry

    lax.fori_loop(0, rows // chunk, one_chunk, 0)


def make_wide(corner, top, edge, vp, per):
    width, chi, cols = top.shape
    legs = 2 * per
    steps = width // legs
    rows = edge.shape[0] // vp
    chunk = min(16, rows)
    depth = legs // per * LANES
    return pl.pallas_call(
        functools.partial(wide_kernel, vp, per, chunk),
        grid=(steps,),
        in_specs=[
            pl.BlockSpec((chi, chi), lambda s: (0, 0)),
            pl.BlockSpec((legs, chi, cols), lambda s: (s, 0, 0)),
            pl.BlockSpec(edge.shape, lambda s: (0, 0)),
        ],
        out_specs=[
            pl.BlockSpec((legs // 2, chi, 2 * cols), lambda s: (s, 0, 0)),
            pl.BlockSpec((rows // 2, depth, 2 * cols), lambda s: (0, s, 0)),
        ],
        out_shape=[
            jax.ShapeDtypeStruct((width // 2, chi, 2 * cols), BF),
            jax.ShapeDtypeStruct((rows // 2, steps * depth, 2 * cols), BF),
        ],
        compiler_params=params(),
        cost_estimate=cost(2 * rows * vp * chi * width * cols, 30e6),
        name="wide",
    )(corner, top, edge)


def place(res, pairs, body, vp, width, store):
    tail = width - body
    base = 2 * pairs * body
    keep = lax.broadcasted_iota(jnp.int32, (2 * tail, LANES), 0) < tail
    for p in range(pairs):
        for side in range(2):
            t = 2 * p + side
            pieces = []
            for i in range(2):
                lo = i * LANES
                pieces.append(res[t * body : (t + 1) * body, lo : lo + LANES])
                last = res[base + 2 * p * tail : base + 2 * (p + 1) * tail, lo : lo + LANES]
                if side:
                    last = pltpu.roll(last, tail, 0)
                pieces.append(jnp.where(keep, last, 0.0))
            store(p, side, jnp.concatenate(pieces, axis=0).astype(BF))


def cut_kernel(width, vp, body, table_ref, wide_ref, proj_ref, cut_ref, quad_ref):
    pairs = quad_ref.shape[0]
    step = pl.program_id(0)
    res = jnp.dot(table_ref[0], wide_ref[0], preferred_element_type=F32)
    at = pl.ds(pl.multiple_of(step * 2 * vp, 16), 2 * vp)

    def store(p, side, value):
        quad_ref[p, at, side * LANES : (side + 1) * LANES] = value

    place(res, pairs, body, vp, width, store)

    @pl.when(step == pl.num_programs(0) - 1)
    def _():
        for p in range(pairs):
            cut_ref[p] = jnp.dot(proj_ref[...], quad_ref[p], preferred_element_type=F32).astype(BF)


def make_cut(table, h, wide, proj_t, width, vp, body):
    count, depth, cols = wide.shape
    chi = proj_t.shape[0]
    pairs = width // 4
    rows = table.shape[1]
    return pl.pallas_call(
        functools.partial(cut_kernel, width, vp, body),
        grid=(count,),
        in_specs=[
            pl.BlockSpec((1, rows, depth), lambda s: (h, 0, 0)),
            pl.BlockSpec((1, depth, cols), lambda s: (s, 0, 0)),
            pl.BlockSpec(proj_t.shape, lambda s: (0, 0)),
        ],
        out_specs=pl.BlockSpec((pairs, chi, cols), lambda s: (0, 0, 0)),
        out_shape=jax.ShapeDtypeStruct((pairs, chi, cols), BF),
        scratch_shapes=[pltpu.VMEM((pairs, count * 2 * vp, cols), BF)],
        compiler_params=params(),
        cost_estimate=cost(2 * count * rows * depth * cols, 30e6),
        name="cut",
    )(table, wide, proj_t)


def quad_kernel(width, vp, body, table_ref, wide_ref, quad_ref):
    pairs = quad_ref.shape[0] // 2
    for h in range(2):
        res = jnp.dot(table_ref[h], wide_ref[0], preferred_element_type=F32)

        def store(p, side, value):
            quad_ref[h * pairs + p, :, side * LANES : (side + 1) * LANES] = value

        place(res, pairs, body, vp, width, store)


def make_quad(table, wide, width, vp, body):
    count, depth, cols = wide.shape
    pairs = width // 2
    return pl.pallas_call(
        functools.partial(quad_kernel, width, vp, body),
        grid=(count,),
        in_specs=[
            pl.BlockSpec(table.shape, lambda s: (0, 0, 0)),
            pl.BlockSpec((1, depth, cols), lambda s: (s, 0, 0)),
        ],
        out_specs=pl.BlockSpec((pairs, 2 * vp, cols), lambda s: (0, s, 0)),
        out_shape=jax.ShapeDtypeStruct((pairs, count * 2 * vp, cols), BF),
        compiler_params=params(),
        cost_estimate=cost(2 * count * width * width * depth * cols, 50e6),
        name="quad",
    )(table, wide)


def half_kernel(scale, quad_ref, first_ref, second_ref, out_ref):
    total = None
    pairs = first_ref.shape[0]
    for p in range(2 * pairs):
        right = first_ref[p] if p < pairs else second_ref[p - pairs]
        term = lax.dot_general(
            quad_ref[p], right, (((1,), (1,)), ((), ())), preferred_element_type=F32
        )
        total = term if total is None else total + term
    out_ref[...] = (total * scale).astype(out_ref.dtype)


def make_half(quad, cuts, begin, rows, dtype, scale):
    pairs, _, cols = quad.shape
    chi = cuts[0].shape[1]
    steps = 2
    block = rows // steps
    return pl.pallas_call(
        functools.partial(half_kernel, scale),
        grid=(steps,),
        in_specs=[
            pl.BlockSpec((pairs, block, cols), lambda s: (0, begin // block + s, 0)),
            pl.BlockSpec(cuts[0].shape, lambda s: (0, 0, 0)),
            pl.BlockSpec(cuts[1].shape, lambda s: (0, 0, 0)),
        ],
        out_specs=pl.BlockSpec((block, chi), lambda s: (s, 0)),
        out_shape=jax.ShapeDtypeStruct((rows, chi), dtype),
        compiler_params=params(),
        cost_estimate=cost(2 * rows * pairs * cols * chi, pairs * rows * cols * 2),
        name="half",
    )(quad, *cuts)


def per_device(
    corner_up, corner_dn, edge_top, edge_bot, edge_up, edge_dn, site_up, site_dn, proj_up, proj_dn
):
    count = lax.axis_size("blk")
    index = lax.axis_index("blk")
    core = index % 2
    side = (index // 2) % 2
    own, width, chi = edge_up.shape[1:]
    span = chi // 2
    vp = round_up(width, 8)
    per = LANES // vp
    body = width // 8 * 8
    far = []
    mask = 4
    while mask < count:
        far.append(mask)
        mask *= 2

    def swap(value, mask):
        return lax.ppermute(value, "blk", [(s, s ^ mask) for s in range(count)])

    def gather(edge):
        local = edge[0].transpose(1, 0, 2)
        keep = lax.dynamic_slice_in_dim(local, side * span, span, 2)
        give = lax.dynamic_slice_in_dim(local, (1 - side) * span, span, 2)
        have = jnp.concatenate([keep, swap(give, 2)], axis=1)
        for mask in far:
            have = jnp.concatenate([have, swap(have, mask)], axis=1)
        return jnp.concatenate([have, swap(have, 1)], axis=1)

    bits = [1] + far[::-1] + [2]

    def reorder(corner):
        value = corner[0].T
        for bit in (mask for mask in [1, 2] + far):
            pairs = value.reshape(count // (2 * bit), 2, bit, own, chi)
            value = jnp.where((index // bit) % 2 == 0, pairs, pairs[:, ::-1])
            value = value.reshape(count * own, chi)
        ways = (2,) * len(bits)
        value = value.reshape(ways + (own, chi))
        natural = sorted(bits, reverse=True)
        value = value.transpose([natural.index(bit) for bit in bits] + [len(bits), len(bits) + 1])
        return value.reshape(chi, chi).T

    def padded(rows):
        rows = jnp.pad(rows.reshape(own, width, chi), ((0, 0), (0, vp - width), (0, 0)))
        return rows.reshape(own * vp, chi)

    def with_partner(value, axis):
        return jnp.concatenate([value, swap(value, 2)], axis=axis)

    bot = gather(edge_bot)
    rows_dn = with_partner(padded(edge_dn[0]), 0)
    proj_dn_t = with_partner(padded(proj_dn[0]).T, 1)
    table_dn = make_table(site_dn[0], vp, per, body)
    grown_dn, wide_dn = make_wide(reorder(corner_dn), bot, rows_dn, vp, per)

    top = gather(edge_top)
    rows_up = with_partner(padded(edge_up[0]), 0)
    proj_up_t = with_partner(padded(proj_up[0]).T, 1)
    table_up = make_table(site_up[0], vp, per, body)

    def reduce_cut(part):
        middle = chi // 2
        keep = lax.dynamic_slice_in_dim(part, core * middle, middle, 1)
        give = lax.dynamic_slice_in_dim(part, (1 - core) * middle, middle, 1)
        total = (keep.astype(F32) + swap(give, 1).astype(F32)).astype(BF)
        for mask in far:
            total = (total.astype(F32) + swap(total, mask).astype(F32)).astype(BF)
        other = swap(total, 1)
        low = jnp.where(core == 0, total, other)
        high = jnp.where(core == 0, other, total)
        return jnp.concatenate([low, high], axis=1)

    cuts = [
        reduce_cut(make_cut(table_dn, h, wide_dn, proj_dn_t, width, vp, body)) for h in range(2)
    ]
    grown_up, wide_up = make_wide(reorder(corner_up), top, rows_up, vp, per)
    quad_up = make_quad(table_up, wide_up, width, vp, body)

    def fresh_part(grown, proj_t):
        mine = lax.dynamic_slice_in_dim(grown, index * own, own, 1)
        theirs = lax.dynamic_slice_in_dim(grown, jnp.bitwise_xor(index, 2) * own, own, 1)
        both = jnp.concatenate([mine, theirs], axis=1).reshape(width // 2, 2 * own, 2, span)
        both = both.transpose(1, 0, 2, 3).reshape(2 * own, width, span)
        both = jnp.pad(both, ((0, 0), (0, vp - width), (0, 0))).reshape(2 * own * vp, span)
        return jnp.dot(proj_t, both, preferred_element_type=F32).astype(BF)

    def spread(part):
        zero = jnp.zeros_like(part)
        return [jnp.where(side == 0, part, zero), jnp.where(side == 0, zero, part)]

    fresh = jnp.concatenate(
        spread(fresh_part(grown_up, proj_up_t)) + spread(fresh_part(grown_dn, proj_dn_t)), axis=1
    )
    fresh = lax.psum_scatter(fresh, "blk", scatter_dimension=0, tiled=True)
    columns = lax.axis_size("col")
    moved = lax.ppermute(fresh, "col", [(s, (s + 1) % columns) for s in range(columns)])

    scale = 1.0 / (chi * width) ** 0.5
    rows = own * vp
    away = make_half(quad_up, cuts, rows, rows, BF, scale)
    arrived = swap(away, 2)
    stay = make_half(quad_up, cuts, 0, rows, F32, scale)
    half = (stay + arrived.astype(F32)).astype(BF)
    half = half.reshape(own, vp, chi)[:, :width].reshape(own * width, chi)
    return (half[None], moved[None, :, :chi], moved[None, :, chi:])


def solution(mesh):
    in_specs = (
        P("col", None, None),
        P("col", None, None),
        P("col", "blk", None, None),
        P("col", "blk", None, None),
        P("col", "blk", None, None),
        P("col", "blk", None, None),
        P("col", None, None, None, None),
        P("col", None, None, None, None),
        P("col", "blk", None),
        P("col", "blk", None),
    )
    out_specs = (P("col", "blk", None), P("col", "blk", None), P("col", "blk", None))
    return jax.shard_map(
        per_device, mesh=mesh, in_specs=in_specs, out_specs=out_specs, check_vma=False
    )
```
